32 devices in a mesh: tensor: 4 (over x, core), request: 8 (over z, y).
Axes of the slice: x: 2, y: 2, z: 4, core: 2. Of those that a mesh axis runs over, the one named last changes fastest.
Arguments:
- hidden_in: bfloat16 [2048, 2048], P('request'), may hold values from -6 to 6
- span_q: bfloat16 [2048, 2048], P('request', 'tensor'), may hold values from -170 to 170
- span_k: bfloat16 [2048, 2048], P('request', 'tensor'), may hold values from -7 to 7
- span_v: bfloat16 [2048, 2048], P('request', 'tensor'), may hold values from -6 to 6
- cache_k: bfloat16 [8, 768, 2048], P('request', None, 'tensor'), may hold values from -6 to 6
- cache_v: bfloat16 [8, 768, 2048], P('request', None, 'tensor'), may hold values from -6 to 6
- cached_len: int32 [8], P('request'), may hold values from 0 to 768
- out_proj: bfloat16 [2048, 2048], P('tensor'), may hold values from -0.125 to 0.125
- norm_gain: float32 [2048], replicated, may hold values from 0.1 to 1.9
- routes: int32 [2048, 4], P('request'), may hold values from 0 to 7, all different within a row; in each aligned block of 256 rows (0 to 255, 256 to 511, ...) at most 256 rows name the same one
- route_weight: float32 [2048, 4], P('request'), may hold values from 0.1 to 1
- w_gate: bfloat16 [8, 2048, 1408], P('request', None, 'tensor'), may hold values from -0.125 to 0.125
- w_up: bfloat16 [8, 2048, 1408], P('request', None, 'tensor'), may hold values from -0.125 to 0.125
- w_down: bfloat16 [8, 1408, 2048], P('request', 'tensor'), may hold values from -0.15625 to 0.15625
Outputs:
- layer_out: bfloat16 [2048, 2048], P('request', 'tensor')
- decode_kv: bfloat16 [8, 2, 1024, 2048], P('request', None, 'tensor')
The draws below stay inside these ranges and needn't reach their ends.
Inputs may be any that keep to these rules, and one draw needn't show every extreme that they name: `routes`: among the rows of one request no expert is named more than 256 times.
All inputs are finite; a program needn't handle non-finite values.
Results may differ from the reference program's by a relative error of at most 0.014.
Values may be sent and summed in bfloat16 or wider, within the bound.
A program may use at most 128 MiB of HBM per device.

```python
import math
import jax
import jax.numpy as jnp
import numpy as np
from jax import lax

D = 2048
HEADS = 16
HD = 128
EXPERT_FF = 1408
TOP = 4
SPAN = 256
PRIOR = 768
REQS = 8
EXPERTS = 8
TOKENS = 2048
CTX = 1024
MOST = 256
N_TENSOR = 4


def span_pair(key):
    base = jax.random.fold_in(key, 101)
    keys = jnp.clip(jax.random.normal(jax.random.fold_in(base, 1), (TOKENS, HEADS * HD), jnp.float32), -6.0, 6.0)
    queries = jnp.clip(jax.random.normal(jax.random.fold_in(base, 2), (TOKENS, HEADS * HD), jnp.float32), -6.0, 6.0)
    return (queries, keys)


def draw_span_q(key, part):
    queries, keys = span_pair(key)
    return queries.astype(jnp.bfloat16)


def draw_span_k(key, part):
    queries, keys = span_pair(key)
    return keys.astype(jnp.bfloat16)


def draw_cached_len(key, part):
    lengths = jax.random.randint(jax.random.fold_in(key, 7), (REQS,), 0, PRIOR + 1)
    longest = jax.random.randint(jax.random.fold_in(key, 8), (), 0, REQS)
    return jnp.where(jnp.arange(REQS) == longest, PRIOR, lengths).astype(jnp.int32)


def block_levels(own_key, extent, split, least, top_value):
    level, own = 1.0, jax.random.fold_in(own_key, 6)
    for dim, blocks in split:
        draws = jnp.exp(jax.random.uniform(jax.random.fold_in(own, dim), (blocks,), jnp.float32, least / len(split), top_value / len(split)))
        level = level * jnp.repeat(draws, extent[dim] // blocks).reshape([-1 if axis == dim else 1 for axis in range(len(extent))])
    return level


def routed_block(stream_key, own, number, rows, number_of, top, bound, slope):
    ranking = jax.random.permutation(stream_key, number_of)
    crowded, usual = portions_of(number_of, rows * top, bound, slope, True), portions_of(number_of, rows * top, bound, slope, False)
    places = jnp.arange(number_of)

    def named(sizes, turn):
        used = int((sizes > 0).sum())
        fixed = max(1, used // 4)
        moved = fixed + (places - fixed + turn * (used - fixed)) % max(1, number_of - fixed)
        return jnp.zeros((number_of,), jnp.int32).at[ranking[jnp.where(places < fixed, places, moved)]].set(jnp.asarray(sizes, jnp.int32))

    sizes = jnp.where(number % 4 == 0, named(crowded, number // 4), named(usual, number - number // 4 - 1))
    mixed = jax.random.permutation(jax.random.fold_in(own, 3), number_of)
    giver, receiver = mixed[0:number_of // 2 * 2:2], mixed[1:number_of // 2 * 2:2]
    room = jnp.minimum(sizes[giver] - 1, bound - sizes[receiver]) // 2
    room = jnp.where((giver == ranking[0]) | (receiver == ranking[0]) | (sizes[receiver] == 0), 0, jnp.maximum(room, 0))
    moved = jax.random.randint(jax.random.fold_in(own, 4), (number_of // 2,), 0, 1 << 20) % (room + 1)
    sizes = sizes.at[giver].add(-moved).at[receiver].add(moved)
    members = jnp.searchsorted(jnp.cumsum(sizes), jnp.arange(rows * top), side="right").astype(jnp.int32)
    grid = members.reshape(top, rows).T
    grid = grid[jax.random.permutation(jax.random.fold_in(own, 1), rows)]
    turn = jax.random.randint(jax.random.fold_in(own, 2), (rows, 1), 0, top)
    return jnp.take_along_axis(grid, (jnp.arange(top)[None, :] + turn) % top, axis=1)


def portions_of(count, total, limit, skew, full):
    loads = [(1 << 20) // math.isqrt(rank ** skew) + 1 for rank in range(1, count + 1)]
    largest = limit if full else min(limit, max(-(-total // count), total * loads[0] // sum(loads)))
    least = 1 if total - largest >= count - 1 else 0
    holding, spare = [largest] + [least] * (count - 1), total - largest - least * (count - 1)
    while spare > 0:
        movable = [i for i in range(1, count) if holding[i] < largest] or [i for i in range(1, count) if holding[i] < limit]
        mass, budget = sum([loads[i] for i in movable]), spare
        for i in movable:
            addition = min(limit - holding[i], max(1, budget * loads[i] // mass), spare)
            holding[i] = holding[i] + addition
            spare = spare - addition
    return np.array(holding)


def scatter_about(rng, extent, scale, reach, cuts=(), kind=jnp.bfloat16):
    factor_of = block_levels(rng, extent, cuts, -0.22, 0.18) if cuts else 1.0
    values = jax.random.normal(rng, extent, jnp.float32) * scale * factor_of
    return jnp.minimum(jnp.maximum(values, -reach), reach).astype(kind)


def setup_inputs(seed: int = 0) -> dict:
    streams_of = jax.random.split(jax.random.key(seed), 15)
    hidden_in = scatter_about(streams_of[0], (TOKENS, D), 1.0, 6.0, ((0, 8),))
    span_q = draw_span_q(jax.random.fold_in(streams_of[14], 71), 0)
    span_k = draw_span_k(jax.random.fold_in(streams_of[14], 71), 0)
    span_v = scatter_about(streams_of[3], (TOKENS, HEADS * HD), 1.0, 6.0, ((0, 8), (1, 4)))
    cache_k = scatter_about(streams_of[4], (REQS, PRIOR, HEADS * HD), 1.0, 6.0, ((0, 8), (2, 4)))
    cache_v = scatter_about(streams_of[5], (REQS, PRIOR, HEADS * HD), 1.0, 6.0, ((0, 8), (2, 4)))
    cached_len = draw_cached_len(jax.random.fold_in(streams_of[14], 71), 0)
    out_proj = scatter_about(streams_of[7], (HEADS * HD, D), (HEADS * HD) ** -0.5, 0.125, ((0, 4),))
    norm_gain = jnp.clip(1.0 + 0.18 * jax.random.normal(streams_of[8], (D,), jnp.float32), 0.1, 1.9)
    routes_keys = jax.random.split(jax.random.fold_in(streams_of[9], 1), TOKENS // SPAN)
    routes_turns = jax.random.permutation(jax.random.fold_in(streams_of[9], 3), TOKENS // SPAN)
    routes = jax.vmap(lambda own, number: routed_block(jax.random.fold_in(streams_of[9], 2), own, number, SPAN, EXPERTS, TOP, MOST, 2))(routes_keys, routes_turns).reshape((TOKENS, TOP))
    route_weight = jnp.clip(jnp.exp(math.log(1.0) - 2.3025851 * jax.random.uniform(streams_of[10], (TOKENS, TOP), jnp.float32) ** block_levels(streams_of[10], (TOKENS, TOP), ((0, 8),), -0.2, 0.2)), 0.1, 1.0)
    w_gate = scatter_about(streams_of[11], (EXPERTS, D, EXPERT_FF), D ** -0.5, 0.125, ((0, 8), (2, 4)))
    w_up = scatter_about(streams_of[12], (EXPERTS, D, EXPERT_FF), D ** -0.5, 0.125, ((0, 8), (2, 4)))
    w_down = scatter_about(streams_of[13], (EXPERTS, EXPERT_FF, D), EXPERT_FF ** -0.5, 0.15625, ((0, 8), (1, 4)))
    return {"hidden_in": hidden_in, "span_q": span_q, "span_k": span_k, "span_v": span_v, "cache_k": cache_k, "cache_v": cache_v, "cached_len": cached_len, "out_proj": out_proj, "norm_gain": norm_gain, "routes": routes, "route_weight": route_weight, "w_gate": w_gate, "w_up": w_up, "w_down": w_down}


eps = 1e-06
neg_large = -1e+30
block_rows = 128

def place(cached, fresh, length):
    positions = jnp.arange(CTX, dtype=jnp.int32)
    padded = jnp.concatenate([cached, jnp.zeros((SPAN, cached.shape[1]), cached.dtype)], axis=0)
    kept = jnp.where((positions < length)[:, None], padded, jnp.zeros_like(padded))
    return lax.dynamic_update_slice(kept, fresh, (length.astype(jnp.int32), jnp.int32(0)))

def reference(hidden_in, span_q, span_k, span_v, cache_k, cache_v, cached_len, out_proj, norm_gain, routes, route_weight, w_gate, w_up, w_down):

    def one_request(index):
        start = (index * SPAN).astype(jnp.int32)
        query = lax.dynamic_slice_in_dim(span_q, start, SPAN, 0)
        new_keys = lax.dynamic_slice_in_dim(span_k, start, SPAN, 0)
        new_values = lax.dynamic_slice_in_dim(span_v, start, SPAN, 0)
        old_keys = lax.dynamic_index_in_dim(cache_k, index, 0, keepdims=False)
        old_values = lax.dynamic_index_in_dim(cache_v, index, 0, keepdims=False)
        length = lax.dynamic_index_in_dim(cached_len, index, 0, keepdims=False)
        keys = jnp.concatenate([old_keys, new_keys], axis=0).reshape(CTX, HEADS, HD)
        values = jnp.concatenate([old_values, new_values], axis=0).reshape(CTX, HEADS, HD)
        scores = jnp.einsum('qhd,khd->hqk', query.reshape(SPAN, HEADS, HD).astype(jnp.float32), keys.astype(jnp.float32)) * HD ** (-0.5)
        key_pos = jnp.arange(CTX, dtype=jnp.int32)[None, :]
        row_pos = jnp.arange(SPAN, dtype=jnp.int32)[:, None]
        valid = jnp.where(key_pos < PRIOR, key_pos < length, key_pos - PRIOR <= row_pos)
        scores = jnp.where(valid[None], scores, neg_large)
        top = lax.optimization_barrier(jnp.max(scores, axis=2, keepdims=True))
        weights = jnp.exp(scores - top)
        probs = (weights / lax.optimization_barrier(jnp.sum(weights, axis=2, keepdims=True))).astype(jnp.bfloat16)
        attended = jnp.einsum('hqk,khd->qhd', probs.astype(jnp.float32), values.astype(jnp.float32)).astype(jnp.bfloat16)
        decode = jnp.stack([place(old_keys, new_keys, length), place(old_values, new_values, length)], axis=0)
        return (attended.reshape(SPAN, HEADS * HD), decode)
    attended, decode_kv = lax.map(one_request, jnp.arange(REQS, dtype=jnp.int32))
    attended = attended.reshape(TOKENS, HEADS * HD)
    mixed = (hidden_in.astype(jnp.float32) + jnp.dot(attended, out_proj, preferred_element_type=jnp.float32)).astype(jnp.bfloat16)
    mixed_f = mixed.astype(jnp.float32)
    normed = (mixed_f * lax.rsqrt(lax.optimization_barrier(jnp.mean(mixed_f * mixed_f, axis=1, keepdims=True)) + eps) * norm_gain).astype(jnp.bfloat16)
    total = TOKENS * TOP
    flat = routes.reshape(-1).astype(jnp.int32)
    onehot = (flat[:, None] == jnp.arange(EXPERTS, dtype=jnp.int32)[None, :]).astype(jnp.int32)
    before = jnp.cumsum(onehot, axis=0) - onehot
    rank = lax.optimization_barrier(jnp.sum(before * onehot, axis=1))
    counts = lax.optimization_barrier(jnp.sum(onehot, axis=0))
    padded_counts = (counts + block_rows - 1) // block_rows * block_rows
    ends = jnp.cumsum(padded_counts)
    starts = ends - padded_counts
    position = starts[flat] + rank
    pad_rows = total + EXPERTS * block_rows
    blocks = pad_rows // block_rows
    source_row = jnp.arange(total, dtype=jnp.int32) // TOP
    buffer = jnp.zeros((pad_rows, D), jnp.bfloat16).at[position].set(normed[source_row])
    block_start = jnp.arange(blocks, dtype=jnp.int32) * block_rows
    block_expert = jnp.minimum(lax.optimization_barrier(jnp.sum((ends[None, :] <= block_start[:, None]).astype(jnp.int32), axis=1)), EXPERTS - 1)
    slice_ff = EXPERT_FF // N_TENSOR

    def expert_block(pair):
        rows, expert = pair
        gate_w = lax.dynamic_index_in_dim(w_gate, expert, 0, keepdims=False)
        up_w = lax.dynamic_index_in_dim(w_up, expert, 0, keepdims=False)
        down_w = lax.dynamic_index_in_dim(w_down, expert, 0, keepdims=False)
        gate = jnp.dot(rows, gate_w, preferred_element_type=jnp.float32)
        upper = jnp.dot(rows, up_w, preferred_element_type=jnp.float32)
        act = (jax.nn.silu(gate) * upper).astype(jnp.bfloat16)
        summed = jnp.zeros((rows.shape[0], D), jnp.float32)
        for piece in range(N_TENSOR):
            part = jnp.dot(act[:, piece * slice_ff:(piece + 1) * slice_ff], down_w[piece * slice_ff:(piece + 1) * slice_ff], preferred_element_type=jnp.float32)
            rounded = lax.optimization_barrier(part.astype(jnp.bfloat16))
            summed = summed + rounded.astype(jnp.float32)
        return summed.astype(jnp.bfloat16)
    results = lax.map(expert_block, (buffer.reshape(blocks, block_rows, D), block_expert))
    expert_out = results.reshape(pad_rows, D)[position].reshape(TOKENS, TOP, D)
    mixture = lax.optimization_barrier(jnp.sum(expert_out.astype(jnp.float32) * route_weight[:, :, None], axis=1))
    layer_out = (mixed_f + mixture).astype(jnp.bfloat16)
    return (layer_out, decode_kv)
```

```python
import jax
import jax.numpy as jnp
from jax import lax
from jax.sharding import PartitionSpec as P

HD = 128
TOP = 4


eps = 1e-06
neg_large = -1e30


def attend(span_q, span_k, span_v, cache_k, cache_v, length):
    span = span_q.shape[0]
    prior = cache_k.shape[1]
    heads = span_q.shape[1] // HD
    keys = jnp.concatenate([cache_k[0], span_k], axis=0).reshape(prior + span, heads, HD)
    values = jnp.concatenate([cache_v[0], span_v], axis=0).reshape(prior + span, heads, HD)
    query = span_q.reshape(span, heads, HD)
    scores = jnp.einsum("qhd,khd->hqk", query, keys, preferred_element_type=jnp.float32) * HD ** (
        -0.5
    )
    key_pos = jnp.arange(prior + span, dtype=jnp.int32)[None, :]
    row_pos = jnp.arange(span, dtype=jnp.int32)[:, None]
    valid = jnp.where(key_pos < prior, key_pos < length, key_pos - prior <= row_pos)
    scores = jnp.where(valid[None], scores, neg_large)
    top = jnp.max(scores, axis=2, keepdims=True)
    weights = jnp.exp(scores - top)
    probs = (weights / jnp.sum(weights, axis=2, keepdims=True)).astype(jnp.bfloat16)
    attended = jnp.einsum("hqk,khd->qhd", probs, values, preferred_element_type=jnp.float32)
    return attended.astype(jnp.bfloat16).reshape(span, heads * HD)


def place(cached, fresh, length, context):
    span = fresh.shape[0]
    positions = jnp.arange(context, dtype=jnp.int32)
    padded = jnp.concatenate([cached[0], jnp.zeros((span, cached.shape[2]), cached.dtype)], axis=0)
    kept = jnp.where((positions < length)[:, None], padded, jnp.zeros_like(padded))
    return lax.dynamic_update_slice(kept, fresh, (length, jnp.int32(0)))


def all_tokens(normed, routes, route_weight, gate_w, up_w, down_w, experts):
    ids = jnp.arange(experts, dtype=jnp.int32)
    spread = jnp.sum(
        jnp.where(routes[:, :, None] == ids, route_weight[:, :, None], 0.0), axis=1
    )
    weights = lax.all_to_all(spread, "request", split_axis=1, concat_axis=0, tiled=True)
    tokens = lax.all_gather(normed, "request", axis=0, tiled=True)
    gate = jnp.dot(tokens, gate_w, preferred_element_type=jnp.float32)
    upper = jnp.dot(tokens, up_w, preferred_element_type=jnp.float32)
    act = (jax.nn.silu(gate) * upper * weights).astype(jnp.bfloat16)
    part = jnp.dot(act, down_w, preferred_element_type=jnp.float32).astype(jnp.bfloat16)
    shares = lax.psum_scatter(part, "tensor", scatter_dimension=1, tiled=True)
    total = lax.psum_scatter(shares, "request", scatter_dimension=0, tiled=True)
    return total.astype(jnp.float32)


def by_slots(normed, routes, route_weight, gate_w, up_w, down_w, experts, most):
    span = normed.shape[0]
    flat = routes.reshape(-1)
    onehot = (flat[:, None] == jnp.arange(experts, dtype=jnp.int32)[None, :]).astype(jnp.float32)
    rows = jnp.arange(span * TOP, dtype=jnp.int32)
    earlier = (rows[None, :] < rows[:, None]).astype(jnp.bfloat16)
    before = jnp.dot(earlier, onehot.astype(jnp.bfloat16), preferred_element_type=jnp.float32)
    slot = jnp.sum(before * onehot, axis=1).astype(jnp.int32)
    dest = (flat * most + slot).reshape(span, TOP)
    slots = jnp.arange(experts * most, dtype=jnp.int32)
    hit = dest[:, :, None] == slots
    send = jnp.any(hit, axis=1).astype(jnp.bfloat16)
    outbox = lax.dot_general(
        send, normed, (((0,), (0,)), ((), ())), preferred_element_type=jnp.float32
    ).astype(jnp.bfloat16)
    inbox = lax.all_to_all(outbox, "request", split_axis=0, concat_axis=0, tiled=True)
    gate = jnp.dot(inbox, gate_w, preferred_element_type=jnp.float32)
    upper = jnp.dot(inbox, up_w, preferred_element_type=jnp.float32)
    act = (jax.nn.silu(gate) * upper).astype(jnp.bfloat16)
    partial_out = jnp.dot(act, down_w, preferred_element_type=jnp.float32)
    shares = lax.psum_scatter(
        partial_out.astype(jnp.bfloat16), "tensor", scatter_dimension=1, tiled=True
    )
    returned = lax.all_to_all(shares, "request", split_axis=0, concat_axis=0, tiled=True)
    weigh = jnp.sum(jnp.where(hit, route_weight[:, :, None], 0.0), axis=1)
    return jnp.dot(weigh, returned.astype(jnp.float32), precision=lax.Precision.HIGHEST)


def on_device(
    hidden_in,
    span_q,
    span_k,
    span_v,
    cache_k,
    cache_v,
    cached_len,
    out_proj,
    norm_gain,
    routes,
    route_weight,
    w_gate,
    w_up,
    w_down,
):
    span, width = hidden_in.shape
    groups = lax.axis_size("tensor")
    quarter = width // groups
    offset = lax.axis_index("tensor") * quarter
    length = cached_len[0]
    attended = attend(span_q, span_k, span_v, cache_k, cache_v, length)
    attn_part = jnp.dot(attended, out_proj, preferred_element_type=jnp.float32)
    attn_full = lax.psum(attn_part.astype(jnp.bfloat16), "tensor").astype(jnp.float32)
    mixed = (hidden_in.astype(jnp.float32) + attn_full).astype(jnp.bfloat16)
    mixed_f = mixed.astype(jnp.float32)
    normed = (
        mixed_f * lax.rsqrt(jnp.mean(mixed_f * mixed_f, axis=1, keepdims=True) + eps) * norm_gain
    ).astype(jnp.bfloat16)
    own_mixed = lax.dynamic_slice_in_dim(mixed, offset, quarter, 1)
    experts = lax.axis_size("request")
    most = max(2, 2 * span * TOP // experts)
    if most >= span:
        mixture = all_tokens(normed, routes, route_weight, w_gate[0], w_up[0], w_down[0], experts)
    else:
        mixture = by_slots(
            normed, routes, route_weight, w_gate[0], w_up[0], w_down[0], experts, most
        )
    layer_out = (own_mixed.astype(jnp.float32) + mixture).astype(jnp.bfloat16)
    context = cache_k.shape[1] + span
    local = jnp.stack(
        [place(cache_k, span_k, length, context), place(cache_v, span_v, length, context)], axis=0
    )[None]
    decode_kv = lax.all_to_all(local, "tensor", split_axis=2, concat_axis=3, tiled=True)
    return (layer_out, decode_kv)


def solution(mesh):
    in_specs = (
        P("request", None),
        P("request", "tensor"),
        P("request", "tensor"),
        P("request", "tensor"),
        P("request", None, "tensor"),
        P("request", None, "tensor"),
        P("request"),
        P("tensor", None),
        P(),
        P("request", None),
        P("request", None),
        P("request", None, "tensor"),
        P("request", None, "tensor"),
        P("request", "tensor", None),
    )
    out_specs = (P("request", "tensor"), P("request", None, "tensor", None))
    return jax.shard_map(
        on_device, mesh=mesh, in_specs=in_specs, out_specs=out_specs, check_vma=False
    )
```

```python
import jax
import jax.numpy as jnp
from jax import lax
from jax.experimental import pallas as pl
from jax.experimental.pallas import tpu as pltpu
from jax.sharding import PartitionSpec as P

HD = 128
TOP = 4


eps = 1e-06
neg_large = -1e30


def attend(span_q, span_k, span_v, cache_k, cache_v, length):
    span = span_q.shape[0]
    prior = cache_k.shape[1]
    heads = span_q.shape[1] // HD
    keys = jnp.concatenate([cache_k[0], span_k], axis=0).reshape(prior + span, heads, HD)
    values = jnp.concatenate([cache_v[0], span_v], axis=0).reshape(prior + span, heads, HD)
    query = span_q.reshape(span, heads, HD)
    scores = jnp.einsum("qhd,khd->hqk", query, keys, preferred_element_type=jnp.float32) * HD ** (
        -0.5
    )
    key_pos = jnp.arange(prior + span, dtype=jnp.int32)[None, :]
    row_pos = jnp.arange(span, dtype=jnp.int32)[:, None]
    valid = jnp.where(key_pos < prior, key_pos < length, key_pos - prior <= row_pos)
    scores = jnp.where(valid[None], scores, neg_large)
    top = jnp.max(scores, axis=2, keepdims=True)
    weights = jnp.exp(scores - top)
    probs = (weights / jnp.sum(weights, axis=2, keepdims=True)).astype(jnp.bfloat16)
    attended = jnp.einsum("hqk,khd->qhd", probs, values, preferred_element_type=jnp.float32)
    return attended.astype(jnp.bfloat16).reshape(span, heads * HD)


def place(cached, fresh, length, context):
    span = fresh.shape[0]
    positions = jnp.arange(context, dtype=jnp.int32)
    padded = jnp.concatenate([cached[0], jnp.zeros((span, cached.shape[2]), cached.dtype)], axis=0)
    kept = jnp.where((positions < length)[:, None], padded, jnp.zeros_like(padded))
    return lax.dynamic_update_slice(kept, fresh, (length, jnp.int32(0)))


MESH = pl.DeviceIdType.MESH
ROWS = 64


def remote(src, dst, send, recv, device):
    return pltpu.make_async_remote_copy(
        src_ref=src,
        dst_ref=dst,
        send_sem=send,
        recv_sem=recv,
        device_id=device,
        device_id_type=MESH,
    )


def position():
    t, r = lax.axis_index("tensor"), lax.axis_index("request")
    x, c, z, y = t // 2, t % 2, r // 2, r % 2
    return t, r, x, c, z, y


def meet(peers):
    barrier = pltpu.get_barrier_semaphore()
    for peer in peers:
        pl.semaphore_signal(barrier, inc=1, device_id=peer, device_id_type=MESH)
    pl.semaphore_wait(barrier, len(peers))


def gather_kernel(
    part, hidden, gain, local, tokens, mixed_out, decode,
    recv_core, chip_sum, recv_x, mixed, normed,
    m_send, m_recv, d_send, d_recv, z_send, z_recv, y_send, y_recv, s_send, s_recv, own_sem,
):
    t, r, x, c, z, y = position()
    span, width = part.shape
    half, quarter = width // 2, width // 4
    depth = decode.shape[1]
    sib = {"tensor": x * 2 + 1 - c}
    across = {"tensor": (1 - x) * 2 + c}
    corner = {"tensor": (1 - x) * 2 + 1 - c}
    beside = {"request": z * 2 + 1 - y}
    line = [{"request": ((z + d) % 4) * 2 + y} for d in (1, 2, 3)]
    meet([sib, across, corner, beside] + line)
    mine = pl.ds(pl.multiple_of(half * c, half), half)
    other = pl.ds(pl.multiple_of(half * (1 - c), half), half)

    core = remote(part.at[:, other], recv_core, m_send.at[0], m_recv.at[0], sib)
    core.start()
    core.wait_recv()

    @pl.loop(0, span // ROWS)
    def _(i):
        rows = pl.ds(pl.multiple_of(i * ROWS, ROWS), ROWS)
        total = part[rows, mine].astype(jnp.float32) + recv_core[rows, :].astype(jnp.float32)
        chip_sum[rows, :] = total.astype(jnp.bfloat16)

    cross = remote(chip_sum, recv_x, m_send.at[1], m_recv.at[1], across)
    cross.start()
    keep = pl.ds(pl.multiple_of(quarter * t, quarter), quarter)
    moves = []
    for j in (1, 2, 3):
        peer = (t + j) % 4
        there = pl.ds(pl.multiple_of(depth * peer, depth), depth)
        moves.append(
            remote(
                local.at[:, there, :], decode.at[:, :, keep], d_send.at[j - 1], d_recv.at[j - 1],
                {"tensor": peer},
            )
        )
        moves[-1].start()
    here = pl.ds(pl.multiple_of(depth * t, depth), depth)
    stay = pltpu.make_async_copy(local.at[:, here, :], decode.at[:, :, keep], own_sem.at[0])
    stay.start()
    cross.wait_recv()

    @pl.loop(0, span // ROWS)
    def _(i):
        rows = pl.ds(pl.multiple_of(i * ROWS, ROWS), ROWS)
        total = chip_sum[rows, :].astype(jnp.float32) + recv_x[rows, :].astype(jnp.float32)
        mixed[rows, mine] = (hidden[rows, mine].astype(jnp.float32) + total).astype(jnp.bfloat16)

    share = remote(mixed.at[:, mine], mixed.at[:, mine], m_send.at[2], m_recv.at[2], sib)
    share.start()
    share.wait_recv()

    @pl.loop(0, span // ROWS)
    def _(i):
        rows = pl.ds(pl.multiple_of(i * ROWS, ROWS), ROWS)
        value = mixed[rows, :].astype(jnp.float32)
        scale = lax.rsqrt(jnp.mean(value * value, axis=1, keepdims=True) + eps)
        normed[rows, :] = (value * scale * gain[...]).astype(jnp.bfloat16)
        mixed_out[rows, :] = mixed[rows, keep]

    own = pltpu.make_async_copy(normed, tokens.at[r], own_sem.at[1])
    own.start()
    zs, ys, ss = [], [], []
    for d in (2, 1, 3):
        zs.append(
            remote(
                normed.at[:, mine], tokens.at[r, :, mine], z_send.at[d - 1], z_recv.at[d - 1],
                line[d - 1],
            )
        )
    ys.append(
        remote(normed.at[:, mine], tokens.at[r, :, mine], y_send.at[0], y_recv.at[0], beside)
    )
    for copy in ys + zs:
        copy.start()

    def to_sib(k, block):
        view = tokens.at[block, :, mine]
        ss.append(remote(view, view, s_send.at[k], s_recv.at[k], sib))
        ss[-1].start()

    ys[0].wait_recv()
    to_sib(0, z * 2 + 1 - y)
    for k, d in enumerate((2, 1, 3)):
        zs[k].wait_recv()
        block = ((z + 4 - d) % 4) * 2 + y
        view = tokens.at[block, :, mine]
        ys.append(remote(view, view, y_send.at[k + 1], y_recv.at[k + 1], beside))
        ys[-1].start()
        to_sib(k + 1, block)
    for k, d in enumerate((2, 1, 3)):
        ys[k + 1].wait_recv()
        to_sib(k + 4, ((z + 4 - d) % 4) * 2 + 1 - y)
    for copy in ss + moves:
        copy.wait_recv()
    for copy in [core, cross, share] + moves + zs + ys + ss:
        copy.wait_send()
    stay.wait()
    own.wait()


def gather_tokens(part, hidden, gain, local, requests):
    span, width = part.shape
    half, quarter = width // 2, width // 4
    context = local.shape[1]
    vmem, anywhere = pl.BlockSpec(memory_space=pltpu.VMEM), pl.BlockSpec(memory_space=pl.ANY)
    dma = pltpu.SemaphoreType.DMA
    return pl.pallas_call(
        gather_kernel,
        out_shape=(
            jax.ShapeDtypeStruct((requests, span, width), jnp.bfloat16),
            jax.ShapeDtypeStruct((span, quarter), jnp.bfloat16),
            jax.ShapeDtypeStruct((2, context // 4, width), jnp.bfloat16),
        ),
        in_specs=[vmem, vmem, vmem, anywhere],
        out_specs=(anywhere, vmem, anywhere),
        scratch_shapes=[pltpu.VMEM((span, half), jnp.bfloat16)] * 3
        + [pltpu.VMEM((span, width), jnp.bfloat16)] * 2
        + [dma((n,)) for n in (3, 3, 3, 3, 3, 3, 4, 4, 7, 7, 2)],
        compiler_params=pltpu.CompilerParams(
            collective_id=0, has_side_effects=True, vmem_limit_bytes=24 << 20
        ),
        name="gather_tokens",
    )(part, hidden, gain, local)


def return_kernel(
    part, out, recv_a, send_x, recv_x, send_y, recv_y, send_z, recv_z, acc,
    a_send, a_recv, x_send, x_recv, y_send, y_recv, z_send, z_recv,
):
    t, r, x, c, z, y = position()
    _, span, width = part.shape
    quarter = width // 4
    sib = {"tensor": x * 2 + 1 - c}
    across = {"tensor": (1 - x) * 2 + c}
    beside = {"request": z * 2 + 1 - y}
    line = [{"request": ((z + d) % 4) * 2 + y} for d in (1, 2, 3)]
    meet([sib, across, beside] + line)

    def columns(xx, cc):
        return pl.ds(pl.multiple_of(quarter * (xx * 2 + cc), quarter), quarter)

    blocks = [((z + d) % 4) * 2 + yy for yy in (1 - y, y) for d in (1, 2, 3, 4)]

    def rows_of(step):
        @pl.loop(0, span // ROWS)
        def _(i):
            step(pl.ds(pl.multiple_of(i * ROWS, ROWS), ROWS))

    firsts, seconds = [], []
    for k, block in enumerate(blocks):
        for copies, j, xx in ((firsts, 0, 1 - x), (seconds, 1, x)):
            copies.append(
                remote(
                    part.at[block, :, columns(xx, 1 - c)], recv_a.at[k, j],
                    a_send.at[k, j], a_recv.at[k, j], sib,
                )
            )
    for copy in firsts + seconds:
        copy.start()
    crossing = []
    for k, block in enumerate(blocks):
        firsts[k].wait_recv()

        def outward(rows, k=k, block=block):
            total = part[block, rows, columns(1 - x, c)].astype(jnp.float32) + recv_a[
                k, 0, rows, :
            ].astype(jnp.float32)
            send_x[k, rows, :] = total.astype(jnp.bfloat16)

        rows_of(outward)
        crossing.append(
            remote(send_x.at[k], recv_x.at[k], x_send.at[k], x_recv.at[k], across)
        )
        crossing[-1].start()
    sides, ends = [], []
    for k, block in enumerate(blocks):
        seconds[k].wait_recv()
        crossing[k].wait_recv()
        if k >= 4:
            sides[k - 4].wait_recv()

        def inward(rows, k=k, block=block):
            total = part[block, rows, columns(x, c)].astype(jnp.float32)
            total = total + recv_a[k, 1, rows, :].astype(jnp.float32)
            total = total + recv_x[k, rows, :].astype(jnp.float32)
            if k < 4:
                send_y[k, rows, :] = total.astype(jnp.bfloat16)
                return
            total = total + recv_y[k - 4, rows, :].astype(jnp.float32)
            if k < 7:
                send_z[k - 4, rows, :] = total.astype(jnp.bfloat16)
            else:
                acc[rows, :] = total

        rows_of(inward)
        if k < 4:
            sides.append(remote(send_y.at[k], recv_y.at[k], y_send.at[k], y_recv.at[k], beside))
            sides[-1].start()
        elif k < 7:
            i = k - 4
            ends.append(remote(send_z.at[i], recv_z.at[i], z_send.at[i], z_recv.at[i], line[i]))
            ends[-1].start()
    for copy in ends:
        copy.wait_recv()

    def finish(rows):
        total = acc[rows, :]
        for i in range(3):
            total = total + recv_z[i, rows, :].astype(jnp.float32)
        out[rows, :] = total

    rows_of(finish)
    for copy in firsts + seconds + crossing + sides + ends:
        copy.wait_send()


def return_sums(part):
    requests, span, width = part.shape
    quarter = width // 4
    vmem = pl.BlockSpec(memory_space=pltpu.VMEM)
    dma = pltpu.SemaphoreType.DMA

    def buffer(*lead):
        return pltpu.VMEM((*lead, span, quarter), jnp.bfloat16)

    return pl.pallas_call(
        return_kernel,
        out_shape=jax.ShapeDtypeStruct((span, quarter), jnp.float32),
        in_specs=[vmem],
        out_specs=vmem,
        scratch_shapes=[
            buffer(8, 2), buffer(8), buffer(8), buffer(4), buffer(4), buffer(3), buffer(3),
            pltpu.VMEM((span, quarter), jnp.float32),
            dma((8, 2)), dma((8, 2)), dma((8,)), dma((8,)), dma((4,)), dma((4,)), dma((3,)), dma((3,)),
        ],
        compiler_params=pltpu.CompilerParams(
            collective_id=1, has_side_effects=True, vmem_limit_bytes=40 << 20
        ),
        name="return_sums",
    )(part)


def all_tokens(tokens, routes, route_weight, gate_w, up_w, down_w):
    experts, span, width = tokens.shape
    ids = jnp.arange(experts, dtype=jnp.int32)
    spread = jnp.sum(
        jnp.where(routes[:, :, None] == ids, route_weight[:, :, None], 0.0), axis=1
    )
    weights = lax.all_to_all(spread, "request", split_axis=1, concat_axis=0, tiled=True)
    tokens = tokens.reshape(experts * span, width)
    gate = jnp.dot(tokens, gate_w, preferred_element_type=jnp.float32)
    upper = jnp.dot(tokens, up_w, preferred_element_type=jnp.float32)
    act = (jax.nn.silu(gate) * upper * weights).astype(jnp.bfloat16)
    part = jnp.dot(act, down_w, preferred_element_type=jnp.float32).astype(jnp.bfloat16)
    return return_sums(part.reshape(experts, span, width))


def by_slots(normed, routes, route_weight, gate_w, up_w, down_w, experts, most):
    span = normed.shape[0]
    flat = routes.reshape(-1)
    onehot = (flat[:, None] == jnp.arange(experts, dtype=jnp.int32)[None, :]).astype(jnp.float32)
    rows = jnp.arange(span * TOP, dtype=jnp.int32)
    earlier = (rows[None, :] < rows[:, None]).astype(jnp.bfloat16)
    before = jnp.dot(earlier, onehot.astype(jnp.bfloat16), preferred_element_type=jnp.float32)
    slot = jnp.sum(before * onehot, axis=1).astype(jnp.int32)
    dest = (flat * most + slot).reshape(span, TOP)
    slots = jnp.arange(experts * most, dtype=jnp.int32)
    hit = dest[:, :, None] == slots
    send = jnp.any(hit, axis=1).astype(jnp.bfloat16)
    outbox = lax.dot_general(
        send, normed, (((0,), (0,)), ((), ())), preferred_element_type=jnp.float32
    ).astype(jnp.bfloat16)
    inbox = lax.all_to_all(outbox, "request", split_axis=0, concat_axis=0, tiled=True)
    gate = jnp.dot(inbox, gate_w, preferred_element_type=jnp.float32)
    upper = jnp.dot(inbox, up_w, preferred_element_type=jnp.float32)
    act = (jax.nn.silu(gate) * upper).astype(jnp.bfloat16)
    partial_out = jnp.dot(act, down_w, preferred_element_type=jnp.float32)
    shares = lax.psum_scatter(
        partial_out.astype(jnp.bfloat16), "tensor", scatter_dimension=1, tiled=True
    )
    returned = lax.all_to_all(shares, "request", split_axis=0, concat_axis=0, tiled=True)
    weigh = jnp.sum(jnp.where(hit, route_weight[:, :, None], 0.0), axis=1)
    return jnp.dot(weigh, returned.astype(jnp.float32), precision=lax.Precision.HIGHEST)


def on_device(
    hidden_in,
    span_q,
    span_k,
    span_v,
    cache_k,
    cache_v,
    cached_len,
    out_proj,
    norm_gain,
    routes,
    route_weight,
    w_gate,
    w_up,
    w_down,
):
    span, width = hidden_in.shape
    groups = lax.axis_size("tensor")
    quarter = width // groups
    offset = lax.axis_index("tensor") * quarter
    length = cached_len[0]
    attended = attend(span_q, span_k, span_v, cache_k, cache_v, length)
    attn_part = jnp.dot(attended, out_proj, preferred_element_type=jnp.float32)
    context = cache_k.shape[1] + span
    local = jnp.stack(
        [place(cache_k, span_k, length, context), place(cache_v, span_v, length, context)], axis=0
    )
    experts = lax.axis_size("request")
    most = max(2, 2 * span * TOP // experts)
    if groups == 4 and experts == 8 and most >= span:
        tokens, own_mixed, decode_kv = gather_tokens(
            attn_part.astype(jnp.bfloat16), hidden_in, norm_gain[None, :], local, experts
        )
        mixture = all_tokens(tokens, routes, route_weight, w_gate[0], w_up[0], w_down[0])
        layer_out = (own_mixed.astype(jnp.float32) + mixture).astype(jnp.bfloat16)
        return (layer_out, decode_kv[None])
    attn_full = lax.psum(attn_part.astype(jnp.bfloat16), "tensor").astype(jnp.float32)
    mixed = (hidden_in.astype(jnp.float32) + attn_full).astype(jnp.bfloat16)
    mixed_f = mixed.astype(jnp.float32)
    normed = (
        mixed_f * lax.rsqrt(jnp.mean(mixed_f * mixed_f, axis=1, keepdims=True) + eps) * norm_gain
    ).astype(jnp.bfloat16)
    own_mixed = lax.dynamic_slice_in_dim(mixed, offset, quarter, 1)
    mixture = by_slots(
        normed, routes, route_weight, w_gate[0], w_up[0], w_down[0], experts, most
    )
    layer_out = (own_mixed.astype(jnp.float32) + mixture).astype(jnp.bfloat16)
    decode_kv = lax.all_to_all(local[None], "tensor", split_axis=2, concat_axis=3, tiled=True)
    return (layer_out, decode_kv)


def solution(mesh):
    in_specs = (
        P("request", None),
        P("request", "tensor"),
        P("request", "tensor"),
        P("request", "tensor"),
        P("request", None, "tensor"),
        P("request", None, "tensor"),
        P("request"),
        P("tensor", None),
        P(),
        P("request", None),
        P("request", None),
        P("request", None, "tensor"),
        P("request", None, "tensor"),
        P("request", "tensor", None),
    )
    out_specs = (P("request", "tensor"), P("request", None, "tensor", None))
    return jax.shard_map(
        on_device, mesh=mesh, in_specs=in_specs, out_specs=out_specs, check_vma=False
    )
```

```python
import jax
import jax.numpy as jnp
from jax import lax
from jax.experimental import pallas as pl
from jax.experimental.pallas import tpu as pltpu
from jax.sharding import PartitionSpec as P

HD = 128
TOP = 4


eps = 1e-06
neg_large = -1e30


def attend(span_q, span_k, span_v, cache_k, cache_v, length):
    span = span_q.shape[0]
    prior = cache_k.shape[1]
    heads = span_q.shape[1] // HD
    keys = jnp.concatenate([cache_k[0], span_k], axis=0).reshape(prior + span, heads, HD)
    values = jnp.concatenate([cache_v[0], span_v], axis=0).reshape(prior + span, heads, HD)
    query = span_q.reshape(span, heads, HD)
    scores = jnp.einsum("qhd,khd->hqk", query, keys, preferred_element_type=jnp.float32) * HD ** (
        -0.5
    )
    key_pos = jnp.arange(prior + span, dtype=jnp.int32)[None, :]
    row_pos = jnp.arange(span, dtype=jnp.int32)[:, None]
    valid = jnp.where(key_pos < prior, key_pos < length, key_pos - prior <= row_pos)
    scores = jnp.where(valid[None], scores, neg_large)
    top = jnp.max(scores, axis=2, keepdims=True)
    weights = jnp.exp(scores - top)
    probs = (weights / jnp.sum(weights, axis=2, keepdims=True)).astype(jnp.bfloat16)
    attended = jnp.einsum("hqk,khd->qhd", probs, values, preferred_element_type=jnp.float32)
    return attended.astype(jnp.bfloat16).reshape(span, heads * HD)


def place(cached, fresh, length, context):
    span = fresh.shape[0]
    positions = jnp.arange(context, dtype=jnp.int32)
    padded = jnp.concatenate([cached[0], jnp.zeros((span, cached.shape[2]), cached.dtype)], axis=0)
    kept = jnp.where((positions < length)[:, None], padded, jnp.zeros_like(padded))
    return lax.dynamic_update_slice(kept, fresh, (length, jnp.int32(0)))


MESH = pl.DeviceIdType.MESH
ROWS = 64
PIECES = 2


def remote(src, dst, send, recv, device):
    return pltpu.make_async_remote_copy(
        src_ref=src,
        dst_ref=dst,
        send_sem=send,
        recv_sem=recv,
        device_id=device,
        device_id_type=MESH,
    )


def position():
    t, r = lax.axis_index("tensor"), lax.axis_index("request")
    x, c, z, y = t // 2, t % 2, r // 2, r % 2
    return t, r, x, c, z, y


def meet(peers):
    barrier = pltpu.get_barrier_semaphore()
    for peer in peers:
        pl.semaphore_signal(barrier, inc=1, device_id=peer, device_id_type=MESH)
    pl.semaphore_wait(barrier, len(peers))


def gather_kernel(
    part, hidden, gain, local, tokens, mixed_out, decode,
    recv_core, chip_sum, recv_x, mixed, normed,
    m_send, m_recv, d_send, d_recv, z_send, z_recv, y_send, y_recv, s_send, s_recv, own_sem,
):
    t, r, x, c, z, y = position()
    span, width = part.shape
    half, quarter = width // 2, width // 4
    depth = decode.shape[1]
    sib = {"tensor": x * 2 + 1 - c}
    across = {"tensor": (1 - x) * 2 + c}
    corner = {"tensor": (1 - x) * 2 + 1 - c}
    beside = {"request": z * 2 + 1 - y}
    line = [{"request": ((z + d) % 4) * 2 + y} for d in (1, 2, 3)]
    meet([sib, across, corner, beside] + line)
    mine = pl.ds(pl.multiple_of(half * c, half), half)
    other = pl.ds(pl.multiple_of(half * (1 - c), half), half)

    core = remote(part.at[:, other], recv_core, m_send.at[0], m_recv.at[0], sib)
    core.start()
    core.wait_recv()

    @pl.loop(0, span // ROWS)
    def _(i):
        rows = pl.ds(pl.multiple_of(i * ROWS, ROWS), ROWS)
        total = part[rows, mine].astype(jnp.float32) + recv_core[rows, :].astype(jnp.float32)
        chip_sum[rows, :] = total.astype(jnp.bfloat16)

    cross = remote(chip_sum, recv_x, m_send.at[1], m_recv.at[1], across)
    cross.start()
    keep = pl.ds(pl.multiple_of(quarter * t, quarter), quarter)
    moves = []
    for j in (1, 2, 3):
        peer = (t + j) % 4
        there = pl.ds(pl.multiple_of(depth * peer, depth), depth)
        moves.append(
            remote(
                local.at[:, there, :], decode.at[:, :, keep], d_send.at[j - 1], d_recv.at[j - 1],
                {"tensor": peer},
            )
        )
        moves[-1].start()
    here = pl.ds(pl.multiple_of(depth * t, depth), depth)
    stay = pltpu.make_async_copy(local.at[:, here, :], decode.at[:, :, keep], own_sem.at[0])
    stay.start()
    cross.wait_recv()

    @pl.loop(0, span // ROWS)
    def _(i):
        rows = pl.ds(pl.multiple_of(i * ROWS, ROWS), ROWS)
        total = chip_sum[rows, :].astype(jnp.float32) + recv_x[rows, :].astype(jnp.float32)
        mixed[rows, mine] = (hidden[rows, mine].astype(jnp.float32) + total).astype(jnp.bfloat16)

    share = remote(mixed.at[:, mine], mixed.at[:, mine], m_send.at[2], m_recv.at[2], sib)
    share.start()
    share.wait_recv()

    @pl.loop(0, span // ROWS)
    def _(i):
        rows = pl.ds(pl.multiple_of(i * ROWS, ROWS), ROWS)
        value = mixed[rows, :].astype(jnp.float32)
        scale = lax.rsqrt(jnp.mean(value * value, axis=1, keepdims=True) + eps)
        normed[rows, :] = (value * scale * gain[...]).astype(jnp.bfloat16)
        mixed_out[rows, :] = mixed[rows, keep]

    own = pltpu.make_async_copy(normed, tokens.at[r], own_sem.at[1])
    own.start()
    zs, ys, ss = [], [], []
    piece = span // PIECES
    bits = [pl.ds(q * piece, piece) for q in range(PIECES)]
    for q, rows in enumerate(bits):
        src, dst = normed.at[rows, mine], tokens.at[r, rows, mine]
        ys.append(remote(src, dst, y_send.at[q, 0], y_recv.at[q, 0], beside))
        ys[-1].start()
        for d in (2, 1, 3):
            zs.append(remote(src, dst, z_send.at[q, d - 1], z_recv.at[q, d - 1], line[d - 1]))
            zs[-1].start()

    def to_sib(q, k, block):
        view = tokens.at[block, bits[q], mine]
        ss.append(remote(view, view, s_send.at[q, k], s_recv.at[q, k], sib))
        ss[-1].start()

    for q, rows in enumerate(bits):
        ys[q].wait_recv()
        to_sib(q, 0, z * 2 + 1 - y)
        for k, d in enumerate((2, 1, 3)):
            zs[3 * q + k].wait_recv()
            block = ((z + 4 - d) % 4) * 2 + y
            view = tokens.at[block, rows, mine]
            ys.append(
                remote(view, view, y_send.at[q, k + 1], y_recv.at[q, k + 1], beside)
            )
            ys[-1].start()
            to_sib(q, k + 1, block)
    for q in range(PIECES):
        for k, d in enumerate((2, 1, 3)):
            ys[PIECES + 3 * q + k].wait_recv()
            to_sib(q, k + 4, ((z + 4 - d) % 4) * 2 + 1 - y)
    for copy in ss + moves:
        copy.wait_recv()
    for copy in [core, cross, share] + moves + zs + ys + ss:
        copy.wait_send()
    stay.wait()
    own.wait()


def gather_tokens(part, hidden, gain, local, requests):
    span, width = part.shape
    half, quarter = width // 2, width // 4
    context = local.shape[1]
    vmem, anywhere = pl.BlockSpec(memory_space=pltpu.VMEM), pl.BlockSpec(memory_space=pl.ANY)
    dma = pltpu.SemaphoreType.DMA
    return pl.pallas_call(
        gather_kernel,
        out_shape=(
            jax.ShapeDtypeStruct((requests, span, width), jnp.bfloat16),
            jax.ShapeDtypeStruct((span, quarter), jnp.bfloat16),
            jax.ShapeDtypeStruct((2, context // 4, width), jnp.bfloat16),
        ),
        in_specs=[vmem, vmem, vmem, anywhere],
        out_specs=(anywhere, vmem, anywhere),
        scratch_shapes=[pltpu.VMEM((span, half), jnp.bfloat16)] * 3
        + [pltpu.VMEM((span, width), jnp.bfloat16)] * 2
        + [dma((n,)) for n in (3, 3, 3, 3)]
        + [dma((PIECES, n)) for n in (3, 3, 4, 4, 7, 7)]
        + [dma((2,))],
        compiler_params=pltpu.CompilerParams(
            collective_id=0, has_side_effects=True, vmem_limit_bytes=24 << 20
        ),
        name="gather_tokens",
    )(part, hidden, gain, local)


def return_kernel(
    part, out, recv_a, send_x, recv_x, send_y, recv_y, send_z, recv_z, acc,
    a_send, a_recv, x_send, x_recv, y_send, y_recv, z_send, z_recv,
):
    t, r, x, c, z, y = position()
    _, span, width = part.shape
    quarter = width // 4
    sib = {"tensor": x * 2 + 1 - c}
    across = {"tensor": (1 - x) * 2 + c}
    beside = {"request": z * 2 + 1 - y}
    line = [{"request": ((z + d) % 4) * 2 + y} for d in (1, 2, 3)]
    meet([sib, across, beside] + line)

    def columns(xx, cc):
        return pl.ds(pl.multiple_of(quarter * (xx * 2 + cc), quarter), quarter)

    blocks = [((z + d) % 4) * 2 + yy for yy in (1 - y, y) for d in (1, 2, 3, 4)]

    def rows_of(step):
        @pl.loop(0, span // ROWS)
        def _(i):
            step(pl.ds(pl.multiple_of(i * ROWS, ROWS), ROWS))

    firsts, seconds = [], []
    for k, block in enumerate(blocks):
        for copies, j, xx in ((firsts, 0, 1 - x), (seconds, 1, x)):
            copies.append(
                remote(
                    part.at[block, :, columns(xx, 1 - c)], recv_a.at[k, j],
                    a_send.at[k, j], a_recv.at[k, j], sib,
                )
            )
    for copy in firsts + seconds:
        copy.start()
    crossing = []
    for k, block in enumerate(blocks):
        firsts[k].wait_recv()

        def outward(rows, k=k, block=block):
            total = part[block, rows, columns(1 - x, c)].astype(jnp.float32) + recv_a[
                k, 0, rows, :
            ].astype(jnp.float32)
            send_x[k, rows, :] = total.astype(jnp.bfloat16)

        rows_of(outward)
        crossing.append(
            remote(send_x.at[k], recv_x.at[k], x_send.at[k], x_recv.at[k], across)
        )
        crossing[-1].start()
    sides, ends = [], []
    for k, block in enumerate(blocks):
        seconds[k].wait_recv()
        crossing[k].wait_recv()
        if k >= 4:
            sides[k - 4].wait_recv()

        def inward(rows, k=k, block=block):
            total = part[block, rows, columns(x, c)].astype(jnp.float32)
            total = total + recv_a[k, 1, rows, :].astype(jnp.float32)
            total = total + recv_x[k, rows, :].astype(jnp.float32)
            if k < 4:
                send_y[k, rows, :] = total.astype(jnp.bfloat16)
                return
            total = total + recv_y[k - 4, rows, :].astype(jnp.float32)
            if k < 7:
                send_z[k - 4, rows, :] = total.astype(jnp.bfloat16)
            else:
                acc[rows, :] = total

        rows_of(inward)
        if k < 4:
            sides.append(remote(send_y.at[k], recv_y.at[k], y_send.at[k], y_recv.at[k], beside))
            sides[-1].start()
        elif k < 7:
            i = k - 4
            ends.append(remote(send_z.at[i], recv_z.at[i], z_send.at[i], z_recv.at[i], line[i]))
            ends[-1].start()
    for copy in ends:
        copy.wait_recv()

    def finish(rows):
        total = acc[rows, :]
        for i in range(3):
            total = total + recv_z[i, rows, :].astype(jnp.float32)
        out[rows, :] = total

    rows_of(finish)
    for copy in firsts + seconds + crossing + sides + ends:
        copy.wait_send()


def return_sums(part):
    requests, span, width = part.shape
    quarter = width // 4
    vmem = pl.BlockSpec(memory_space=pltpu.VMEM)
    dma = pltpu.SemaphoreType.DMA

    def buffer(*lead):
        return pltpu.VMEM((*lead, span, quarter), jnp.bfloat16)

    return pl.pallas_call(
        return_kernel,
        out_shape=jax.ShapeDtypeStruct((span, quarter), jnp.float32),
        in_specs=[vmem],
        out_specs=vmem,
        scratch_shapes=[
            buffer(8, 2), buffer(8), buffer(8), buffer(4), buffer(4), buffer(3), buffer(3),
            pltpu.VMEM((span, quarter), jnp.float32),
            dma((8, 2)), dma((8, 2)), dma((8,)), dma((8,)), dma((4,)), dma((4,)), dma((3,)), dma((3,)),
        ],
        compiler_params=pltpu.CompilerParams(
            collective_id=1, has_side_effects=True, vmem_limit_bytes=40 << 20
        ),
        name="return_sums",
    )(part)


def all_tokens(tokens, routes, route_weight, gate_w, up_w, down_w):
    experts, span, width = tokens.shape
    ids = jnp.arange(experts, dtype=jnp.int32)
    spread = jnp.sum(
        jnp.where(routes[:, :, None] == ids, route_weight[:, :, None], 0.0), axis=1
    )
    weights = lax.all_to_all(spread, "request", split_axis=1, concat_axis=0, tiled=True)
    tokens = tokens.reshape(experts * span, width)
    gate = jnp.dot(tokens, gate_w, preferred_element_type=jnp.float32)
    upper = jnp.dot(tokens, up_w, preferred_element_type=jnp.float32)
    act = (jax.nn.silu(gate) * upper * weights).astype(jnp.bfloat16)
    part = jnp.dot(act, down_w, preferred_element_type=jnp.float32).astype(jnp.bfloat16)
    return return_sums(part.reshape(experts, span, width))


def by_slots(normed, routes, route_weight, gate_w, up_w, down_w, experts, most):
    span = normed.shape[0]
    flat = routes.reshape(-1)
    onehot = (flat[:, None] == jnp.arange(experts, dtype=jnp.int32)[None, :]).astype(jnp.float32)
    rows = jnp.arange(span * TOP, dtype=jnp.int32)
    earlier = (rows[None, :] < rows[:, None]).astype(jnp.bfloat16)
    before = jnp.dot(earlier, onehot.astype(jnp.bfloat16), preferred_element_type=jnp.float32)
    slot = jnp.sum(before * onehot, axis=1).astype(jnp.int32)
    dest = (flat * most + slot).reshape(span, TOP)
    slots = jnp.arange(experts * most, dtype=jnp.int32)
    hit = dest[:, :, None] == slots
    send = jnp.any(hit, axis=1).astype(jnp.bfloat16)
    outbox = lax.dot_general(
        send, normed, (((0,), (0,)), ((), ())), preferred_element_type=jnp.float32
    ).astype(jnp.bfloat16)
    inbox = lax.all_to_all(outbox, "request", split_axis=0, concat_axis=0, tiled=True)
    gate = jnp.dot(inbox, gate_w, preferred_element_type=jnp.float32)
    upper = jnp.dot(inbox, up_w, preferred_element_type=jnp.float32)
    act = (jax.nn.silu(gate) * upper).astype(jnp.bfloat16)
    partial_out = jnp.dot(act, down_w, preferred_element_type=jnp.float32)
    shares = lax.psum_scatter(
        partial_out.astype(jnp.bfloat16), "tensor", scatter_dimension=1, tiled=True
    )
    returned = lax.all_to_all(shares, "request", split_axis=0, concat_axis=0, tiled=True)
    weigh = jnp.sum(jnp.where(hit, route_weight[:, :, None], 0.0), axis=1)
    return jnp.dot(weigh, returned.astype(jnp.float32), precision=lax.Precision.HIGHEST)


def on_device(
    hidden_in,
    span_q,
    span_k,
    span_v,
    cache_k,
    cache_v,
    cached_len,
    out_proj,
    norm_gain,
    routes,
    route_weight,
    w_gate,
    w_up,
    w_down,
):
    span, width = hidden_in.shape
    groups = lax.axis_size("tensor")
    quarter = width // groups
    offset = lax.axis_index("tensor") * quarter
    length = cached_len[0]
    attended = attend(span_q, span_k, span_v, cache_k, cache_v, length)
    attn_part = jnp.dot(attended, out_proj, preferred_element_type=jnp.float32)
    context = cache_k.shape[1] + span
    local = jnp.stack(
        [place(cache_k, span_k, length, context), place(cache_v, span_v, length, context)], axis=0
    )
    experts = lax.axis_size("request")
    most = max(2, 2 * span * TOP // experts)
    if groups == 4 and experts == 8 and most >= span:
        tokens, own_mixed, decode_kv = gather_tokens(
            attn_part.astype(jnp.bfloat16), hidden_in, norm_gain[None, :], local, experts
        )
        mixture = all_tokens(tokens, routes, route_weight, w_gate[0], w_up[0], w_down[0])
        layer_out = (own_mixed.astype(jnp.float32) + mixture).astype(jnp.bfloat16)
        return (layer_out, decode_kv[None])
    attn_full = lax.psum(attn_part.astype(jnp.bfloat16), "tensor").astype(jnp.float32)
    mixed = (hidden_in.astype(jnp.float32) + attn_full).astype(jnp.bfloat16)
    mixed_f = mixed.astype(jnp.float32)
    normed = (
        mixed_f * lax.rsqrt(jnp.mean(mixed_f * mixed_f, axis=1, keepdims=True) + eps) * norm_gain
    ).astype(jnp.bfloat16)
    own_mixed = lax.dynamic_slice_in_dim(mixed, offset, quarter, 1)
    mixture = by_slots(
        normed, routes, route_weight, w_gate[0], w_up[0], w_down[0], experts, most
    )
    layer_out = (own_mixed.astype(jnp.float32) + mixture).astype(jnp.bfloat16)
    decode_kv = lax.all_to_all(local[None], "tensor", split_axis=2, concat_axis=3, tiled=True)
    return (layer_out, decode_kv)


def solution(mesh):
    in_specs = (
        P("request", None),
        P("request", "tensor"),
        P("request", "tensor"),
        P("request", "tensor"),
        P("request", None, "tensor"),
        P("request", None, "tensor"),
        P("request"),
        P("tensor", None),
        P(),
        P("request", None),
        P("request", None),
        P("request", None, "tensor"),
        P("request", None, "tensor"),
        P("request", "tensor", None),
    )
    out_specs = (P("request", "tensor"), P("request", None, "tensor", None))
    return jax.shard_map(
        on_device, mesh=mesh, in_specs=in_specs, out_specs=out_specs, check_vma=False
    )
```
